128 devices in a mesh: replica: 8 (over z, core), fsdp: 16 (over y, x).
Axes of the slice: x: 4, y: 4, z: 4, core: 2. Of those that a mesh axis runs over, the one named last changes fastest.
Arguments:
- grads: bfloat16 [8, 8192, 4096], P('replica', 'fsdp'), may hold values from -6 to 6
- owners: int32 [16, 8], P(None, 'replica'), may hold values from 0 to 31, as said below
- factors: bfloat16 [8, 16, 2, 2, 512, 512], P('replica', 'fsdp'), as said below
- momentum: bfloat16 [8, 16, 2, 512, 512], P('replica', 'fsdp'), may hold values from -6 to 6
- accum: float32 [8, 16, 2, 512, 512], P('replica', 'fsdp'), may hold values from 0.1 to 10
Outputs:
- update: bfloat16 [8192, 4096], P('fsdp')
- momentum_out: bfloat16 [8, 16, 2, 512, 512], P('replica', 'fsdp')
- accum_out: float32 [8, 16, 2, 512, 512], P('replica', 'fsdp')
The draws below stay inside these ranges and needn't reach their ends.
Inputs may be any that keep to these rules, and one draw needn't show every extreme that they name: `owners`: each entry is f * 2 + s: slot s of fsdp index f within the replica index that holds the block's columns. Within one replica index no slot is named twice, some fsdp index has all 2 of its slots named, and both the first and the last slot are named. Each of the two factors of a slot is symmetric and positive definite.
All inputs are finite; a program needn't handle non-finite values.
Results may differ from the reference program's by a relative error of at most 0.029.
Values may be sent and summed in bfloat16 or wider, within the bound.
No kernel may reach another device: no remote copies, remote signals or barrier semaphores. Data moves between devices by JAX's collectives and lax.ppermute only.
A program may use at most 128 MiB of HBM per device.

```python
import math
import jax
import jax.numpy as jnp
from jax import lax

D = 8192
COLS = 4096
B = 512
SLOTS = 2
N_REPLICA = 8
N_FSDP = 16


def draw_owners(key, part):
    key = jax.random.fold_in(key, 11)
    nrow = D // B
    group_cols = COLS // B // N_REPLICA
    group = nrow * group_cols
    total = N_FSDP * SLOTS

    def one_group(sub):
        first, second, third = jax.random.split(sub, 3)
        filled = jax.random.randint(first, (), 0, N_FSDP)
        slot_ids = jnp.arange(total, dtype=jnp.int32)
        ranking = jax.random.permutation(second, total).astype(jnp.int32)
        at_ends = (slot_ids == 0) | (slot_ids == total - 1)
        scores = jnp.where(slot_ids // SLOTS == filled, slot_ids - 2 * total, jnp.where(at_ends, slot_ids - total, ranking))
        chosen = jnp.argsort(scores, stable=True)[:group].astype(jnp.int32)
        return jax.random.permutation(third, chosen).astype(jnp.int32)
    values = jax.vmap(one_group)(jax.random.split(key, N_REPLICA))
    values = values.reshape(N_REPLICA, nrow, group_cols).transpose(1, 0, 2)
    return values.reshape(nrow, N_REPLICA * group_cols).astype(jnp.int32)


def draw_factors(key, part):
    key = jax.random.fold_in(key, 5)
    first, second = jax.random.split(key)
    shape = (N_REPLICA, N_FSDP, SLOTS, 2, B, B)
    noise = jax.random.normal(first, shape, jnp.float32)
    symmetric = (noise + jnp.swapaxes(noise, -1, -2)) * (0.2 * B ** (-0.5))
    diagonal = jnp.exp(jax.random.uniform(second, shape[:-1], jnp.float32, 0.0, math.log(3.0)))
    rows = jnp.arange(B)
    identity = (rows[:, None] == rows[None, :]).astype(jnp.float32)
    return (symmetric + identity * diagonal[..., None]).astype(jnp.bfloat16)


def spiked(values, own_key, source, target, shards_of, factor):
    def block_of(position):
        return (jnp.arange(values.shape[position]) // (values.shape[position] // shards_of)).reshape((-1,) + (1,) * (values.ndim - 1 - position))

    near = jax.random.permutation(own_key, shards_of)[block_of(target)]
    far = (block_of(target) + shards_of // 2) % shards_of
    return jnp.where((block_of(source) == near) | (block_of(source) == far), factor * values, values)


def steps_of(rng, dims, cuts, smallest, high):
    gain, own = 1.0, jax.random.fold_in(rng, 6)
    for position, blocks in cuts:
        steps = jnp.exp(jax.random.uniform(jax.random.fold_in(own, position), (blocks,), jnp.float32, smallest / len(cuts), high / len(cuts)))
        gain = gain * jnp.repeat(steps, dims[position] // blocks).reshape([-1 if axis == position else 1 for axis in range(len(dims))])
    return gain


def normal_values(stream_key, dims, spread, bound, pieces=(), kind=jnp.bfloat16):
    array = spread * jax.random.normal(stream_key, dims, jnp.float32)
    if pieces:
        array = array * steps_of(stream_key, dims, pieces, -0.22, 0.18)
    return jnp.clip(array, -bound, bound).astype(kind)


def gaussian_with(stream_key, dims, width, most, cuts, heavy, kind=jnp.bfloat16):
    array = width * jax.random.normal(stream_key, dims, jnp.float32)
    if cuts:
        array = array * steps_of(stream_key, dims, cuts, -0.22, 0.18)
    return jnp.clip(spiked(array, jax.random.fold_in(stream_key, 3), *heavy), -most, most).astype(kind)


def setup_inputs(seed: int = 0) -> dict:
    seeds = jax.random.split(jax.random.key(seed), 6)
    return {
        "grads": gaussian_with(seeds[0], (N_REPLICA, D, COLS), 1.0, 6.0, ((0, 8), (1, 16)), (0, 2, 8, 2.0)),
        "owners": draw_owners(jax.random.fold_in(seeds[5], 71), 0),
        "factors": draw_factors(jax.random.fold_in(seeds[5], 71), 0),
        "momentum": normal_values(seeds[3], (N_REPLICA, N_FSDP, SLOTS, B, B), 1.0, 6.0, ((0, 8), (1, 16))),
        "accum": jnp.clip(jnp.exp(math.log(10.0) - 4.6051702 * jax.random.uniform(seeds[4], (N_REPLICA, N_FSDP, SLOTS, B, B), jnp.float32) ** steps_of(seeds[4], (N_REPLICA, N_FSDP, SLOTS, B, B), ((0, 8), (1, 16)), -0.2, 0.2)), 0.1, 10.0),
    }


def slot_step(grad_block, left, right, moment, squares):
    grad_f = grad_block.astype(jnp.float32)
    squares_new = squares + grad_f * grad_f
    adagrad = grad_f / jnp.sqrt(squares_new)
    inner = jnp.dot(left.astype(jnp.float32), grad_f, precision=lax.Precision.HIGHEST)
    precond = jnp.dot(inner, right.astype(jnp.float32), precision=lax.Precision.HIGHEST)
    ratio = jnp.sqrt(jnp.sum(adagrad * adagrad)) / jnp.sqrt(jnp.sum(precond * precond) + 1e-06)
    step = precond * ratio
    moment_new = (0.9 * moment.astype(jnp.float32) + step).astype(jnp.bfloat16)
    kept = lax.optimization_barrier(moment_new)
    update = (0.9 * kept.astype(jnp.float32) + step).astype(jnp.bfloat16)
    return (moment_new, squares_new, update)

def reference(grads, owners, factors, momentum, accum):
    nrow = D // B
    ncol = COLS // B
    group_cols = ncol // N_REPLICA
    gradient = lax.optimization_barrier(jnp.sum(grads.astype(jnp.float32), axis=0)).astype(jnp.bfloat16)
    blocks = gradient.reshape(nrow, B, ncol, B).transpose(0, 2, 1, 3).reshape(nrow * ncol, B, B)
    col_index = jnp.arange(ncol, dtype=jnp.int32)
    group = col_index // group_cols
    slot_global = (group[None, :] * (N_FSDP * SLOTS) + owners).reshape(nrow * ncol).astype(jnp.int32)
    total_slots = N_REPLICA * N_FSDP * SLOTS
    flat_factors = factors.reshape(total_slots, 2, B, B)
    flat_moment = momentum.reshape(total_slots, B, B)
    flat_squares = accum.reshape(total_slots, B, B)

    def one_block(item):
        grad_block, slot = item
        return slot_step(grad_block, flat_factors[slot, 0], flat_factors[slot, 1], flat_moment[slot], flat_squares[slot])
    moment_new, squares_new, updates = lax.map(one_block, (blocks, slot_global))
    base_moment = (0.9 * flat_moment.astype(jnp.float32) + 0.0).astype(jnp.bfloat16)
    momentum_out = base_moment.at[slot_global].set(moment_new).reshape(momentum.shape)
    accum_out = flat_squares.at[slot_global].set(squares_new).reshape(accum.shape)
    update = updates.reshape(nrow, ncol, B, B).transpose(0, 2, 1, 3).reshape(D, COLS)
    return (update, momentum_out, accum_out)
```

```python
import jax
import jax.numpy as jnp
from jax import lax
from jax.experimental import pallas as pl
from jax.experimental.pallas import tpu as pltpu
from jax.sharding import PartitionSpec as P

SIDE = 512
SLOTS = 2
PEERS = 16
PIECE = SIDE // PEERS
HALF = SIDE // 2
VMEM_LIMIT = 48 * 1024 * 1024


def ring(step):
    return [(i, ((i // 2 + step) % 4) * 2 + i % 2) for i in range(8)]


UP = ring(1)
DOWN = ring(3)
CORES = [(i, i ^ 1) for i in range(8)]


def add(a, b):
    return (a.astype(jnp.float32) + b.astype(jnp.float32)).astype(jnp.bfloat16)


def sum_replicas(grads, z, core):
    def part(d, which):
        col = (lax.rem(z + d, 4) * 2 + which) * SIDE
        return lax.dynamic_slice(grads, (0, col), (SIDE, SIDE))

    give = jnp.stack([part(d, 1 - core) for d in (2, 1, 3, 0)])
    got = lax.ppermute(give, "replica", CORES)
    s = {d: add(part(d, core), got[n]) for n, d in enumerate((2, 1, 3, 0))}
    up1 = lax.ppermute(s[2][:HALF], "replica", UP)
    down1 = lax.ppermute(s[2][HALF:], "replica", DOWN)
    up2 = lax.ppermute(s[1][HALF:], "replica", UP)
    down2 = lax.ppermute(s[3][:HALF], "replica", DOWN)
    up3 = lax.ppermute(add(s[1][:HALF], up1), "replica", UP)
    down3 = lax.ppermute(add(s[3][HALF:], down1), "replica", DOWN)
    own = s[0].astype(jnp.float32)
    top = own[:HALF] + down2.astype(jnp.float32) + up3.astype(jnp.float32)
    low = own[HALF:] + up2.astype(jnp.float32) + down3.astype(jnp.float32)
    return jnp.concatenate([top, low]).astype(jnp.bfloat16)


def pick_kernel(index_ref, x_ref, o_ref):
    for t in range(o_ref.shape[0]):
        i = index_ref[t]
        v = x_ref[jnp.maximum(i, 0)]
        o_ref[t] = jnp.where(i >= 0, v, jnp.zeros_like(v))


def pick(index, x, count):
    return pl.pallas_call(
        pick_kernel,
        out_shape=jax.ShapeDtypeStruct((count,) + x.shape[1:], x.dtype),
        in_specs=[
            pl.BlockSpec(memory_space=pltpu.SMEM),
            pl.BlockSpec(memory_space=pltpu.VMEM),
        ],
        out_specs=pl.BlockSpec(memory_space=pltpu.VMEM),
        compiler_params=pltpu.CompilerParams(vmem_limit_bytes=VMEM_LIMIT),
        name="pick",
    )(index, x)


def slot_kernel(g_ref, f_ref, m_ref, a_ref, mo_ref, ao_ref, u_ref):
    g = g_ref[...].reshape(SIDE, SIDE)
    gf = g.astype(jnp.float32)
    squares = gf * gf
    accum = a_ref[0] + squares
    ao_ref[0] = accum
    adagrad = jnp.sum(squares / accum)
    inner = jnp.dot(f_ref[0, 0], g, preferred_element_type=jnp.float32)
    precond = jnp.dot(
        inner.astype(jnp.bfloat16), f_ref[0, 1], preferred_element_type=jnp.float32
    )
    norm = jnp.sum(precond * precond) + 1e-06
    step = precond * (jnp.sqrt(adagrad) / jnp.sqrt(norm))
    moment = (0.9 * m_ref[0].astype(jnp.float32) + step).astype(jnp.bfloat16)
    mo_ref[0] = moment
    update = (0.9 * moment.astype(jnp.float32) + step).astype(jnp.bfloat16)
    u_ref[...] = update.reshape(u_ref.shape)


def slot_step(g, factors, momentum, accum):
    block = (1, SIDE, SIDE)
    pieces = pl.BlockSpec((PEERS, 1, PIECE, SIDE), lambda s: (0, s, 0, 0))
    flat = pl.BlockSpec(block, lambda s: (s, 0, 0))
    return pl.pallas_call(
        slot_kernel,
        grid=(SLOTS,),
        out_shape=(
            jax.ShapeDtypeStruct(momentum.shape, momentum.dtype),
            jax.ShapeDtypeStruct(accum.shape, accum.dtype),
            jax.ShapeDtypeStruct(g.shape, jnp.bfloat16),
        ),
        in_specs=[
            pieces,
            pl.BlockSpec((1, 2, SIDE, SIDE), lambda s: (s, 0, 0, 0)),
            flat,
            flat,
        ],
        out_specs=(flat, flat, pieces),
        compiler_params=pltpu.CompilerParams(vmem_limit_bytes=VMEM_LIMIT),
        name="slot_step",
    )(g, factors, momentum, accum)


def gather_replicas(tile, z, core):
    top, low = tile[:HALF], tile[HALF:]
    own = lax.ppermute(tile, "replica", CORES)
    up1 = lax.ppermute(top, "replica", UP)
    down1 = lax.ppermute(low, "replica", DOWN)
    up2 = lax.ppermute(low, "replica", UP)
    down2 = lax.ppermute(top, "replica", DOWN)
    up3 = lax.ppermute(up1, "replica", UP)
    down3 = lax.ppermute(down1, "replica", DOWN)
    out = jnp.zeros((SIDE, 8 * SIDE), tile.dtype)
    for d, pair in ((3, (up1, up2)), (1, (down2, down1)), (2, (up3, down3))):
        col = lax.rem(z + d, 4) * 2 * SIDE
        for n, half in enumerate(pair):
            other = lax.ppermute(half, "replica", CORES)
            out = lax.dynamic_update_slice(out, half, (n * HALF, col + core * SIDE))
            out = lax.dynamic_update_slice(out, other, (n * HALF, col + (1 - core) * SIDE))
    out = lax.dynamic_update_slice(out, tile, (0, z * 2 * SIDE + core * SIDE))
    return lax.dynamic_update_slice(out, own, (0, z * 2 * SIDE + (1 - core) * SIDE))


def body(grads, owners, factors, momentum, accum):
    replica = lax.axis_index("replica")
    z, core = replica // 2, lax.rem(replica, 2)
    ids = owners[:, 0]
    named = ids[None, :] == jnp.arange(PEERS * SLOTS, dtype=jnp.int32)[:, None]
    block_of = jnp.max(
        jnp.where(named, jnp.arange(PEERS, dtype=jnp.int32)[None, :], -1), axis=1
    )

    home = sum_replicas(grads[0], z, core)
    pieces = lax.all_to_all(home.reshape(PEERS, PIECE, SIDE), "fsdp", 0, 0, tiled=True)
    routed = pick(block_of, pieces, PEERS * SLOTS)
    slot_grad = lax.all_to_all(
        routed.reshape(PEERS, SLOTS, PIECE, SIDE), "fsdp", 0, 0, tiled=True
    )
    moment_new, squares_new, update = slot_step(
        slot_grad, factors[0, 0], momentum[0, 0], accum[0, 0]
    )
    back = lax.all_to_all(update, "fsdp", 0, 0, tiled=True)
    back = pick(ids, back.reshape(PEERS * SLOTS, PIECE, SIDE), PEERS)
    tile = lax.all_to_all(back, "fsdp", 0, 0, tiled=True).reshape(SIDE, SIDE)
    out = gather_replicas(tile, z, core)
    return (out, moment_new[None, None], squares_new[None, None])


def solution(mesh):
    in_specs = (
        P("replica", "fsdp", None),
        P(None, "replica"),
        P("replica", "fsdp", None, None, None, None),
        P("replica", "fsdp", None, None, None),
        P("replica", "fsdp", None, None, None),
    )
    out_specs = (
        P("fsdp", None),
        P("replica", "fsdp", None, None, None),
        P("replica", "fsdp", None, None, None),
    )
    return jax.shard_map(body, mesh=mesh, in_specs=in_specs, out_specs=out_specs, check_vma=False)
```

```python
import jax
import jax.numpy as jnp
from jax import lax
from jax.experimental import pallas as pl
from jax.experimental.pallas import tpu as pltpu
from jax.sharding import PartitionSpec as P

SIDE = 512
SLOTS = 2
PEERS = 16
PIECE = SIDE // PEERS
HALF = SIDE // 2
VMEM_LIMIT = 24 * 1024 * 1024


def ring(step):
    return [(i, ((i // 2 + step) % 4) * 2 + i % 2) for i in range(8)]


UP = ring(1)
DOWN = ring(3)
CORES = [(i, i ^ 1) for i in range(8)]


def add(a, b):
    return (a.astype(jnp.float32) + b.astype(jnp.float32)).astype(jnp.bfloat16)


def vmem_call(kernel, name, out_shape, *operands):
    spec = pl.BlockSpec(memory_space=pltpu.VMEM)
    return pl.pallas_call(
        kernel,
        out_shape=out_shape,
        in_specs=[spec] * len(operands),
        out_specs=jax.tree.map(lambda _: spec, out_shape),
        compiler_params=pltpu.CompilerParams(vmem_limit_bytes=VMEM_LIMIT),
        name=name,
    )(*operands)


def swap(x):
    with jax.named_scope("swap"):
        return lax.ppermute(x, "replica", CORES)


def up(x, name):
    with jax.named_scope(name):
        return lax.ppermute(x, "replica", UP)


def down(x, name):
    with jax.named_scope(name):
        return lax.ppermute(x, "replica", DOWN)


def home_kernel(a_ref, t1_ref, t2_ref, l1_ref, l2_ref, o_ref):
    for n, (x_ref, y_ref) in enumerate(((t1_ref, t2_ref), (l1_ref, l2_ref))):
        rows = pl.ds(n * HALF, HALF)
        total = a_ref[rows] + x_ref[...].astype(jnp.float32) + y_ref[...].astype(jnp.float32)
        o_ref[rows] = total.astype(jnp.bfloat16)


def sum_replicas(grads, z, core, extra):
    def part(x, d, which):
        col = (lax.rem(z + d, 4) * 2 + which) * SIDE
        return lax.dynamic_slice(x, (0, col), (SIDE, SIDE))

    def halves(x):
        x = x.astype(jnp.bfloat16)
        return x[:HALF], x[HALF:]

    def both(x, d, got):
        return part(x, d, core).astype(jnp.float32) + got.astype(jnp.float32)

    give2 = part(grads, 2, 1 - core)
    later, give2 = lax.optimization_barrier((grads, give2))
    got2 = swap(give2)
    got1, got3, got0 = (swap(part(later, d, 1 - core)) for d in (1, 3, 0))
    s2 = both(later, 2, got2).astype(jnp.bfloat16)
    later, s2, extra = lax.optimization_barrier((later, s2, extra))
    top2, low2 = halves(s2)
    up1, down1 = up(top2, "up1"), down(low2, "down1")
    top1, low1 = halves(both(later, 1, got1))
    top3, low3 = halves(both(later, 3, got3))
    up2, down2 = up(low1, "up2"), down(top3, "down2")
    up3, down3 = up(add(top1, up1), "up3"), down(add(low3, down1), "down3")
    shape = jax.ShapeDtypeStruct((SIDE, SIDE), jnp.bfloat16)
    home = vmem_call(home_kernel, "home", shape, both(later, 0, got0), down2, up3, up2, down3)
    return home, extra


def pick_kernel(index_ref, x_ref, o_ref):
    for t in range(o_ref.shape[0]):
        i = index_ref[t]
        v = x_ref[jnp.maximum(i, 0)]
        o_ref[t] = jnp.where(i >= 0, v, jnp.zeros_like(v))


def pick(index, x, count):
    return pl.pallas_call(
        pick_kernel,
        out_shape=jax.ShapeDtypeStruct((count,) + x.shape[1:], x.dtype),
        in_specs=[
            pl.BlockSpec(memory_space=pltpu.SMEM),
            pl.BlockSpec(memory_space=pltpu.VMEM),
        ],
        out_specs=pl.BlockSpec(memory_space=pltpu.VMEM),
        compiler_params=pltpu.CompilerParams(vmem_limit_bytes=VMEM_LIMIT),
        name="pick",
    )(index, x)


def tile_sum(x):
    return jnp.sum(x.reshape(-1, 8, SIDE), axis=0)


def slot_kernel(
    g_ref, f_ref, m_ref, a_hbm, mo_hbm, ao_hbm, u_ref,
    a_ref, ao_ref, mo_ref, p_ref, i_ref, a_sem, ao_sem, mo_sem,
):
    slots = range(SLOTS)
    a_in = [pltpu.make_async_copy(a_hbm.at[s], a_ref.at[s], a_sem.at[s]) for s in slots]
    a_out = [pltpu.make_async_copy(ao_ref.at[s], ao_hbm.at[s], ao_sem.at[s]) for s in slots]
    m_out = [pltpu.make_async_copy(mo_ref.at[s], mo_hbm.at[s], mo_sem.at[s]) for s in slots]
    for s in slots:
        a_in[s].start()
    for s in slots:
        g = g_ref[:, s].reshape(SIDE, SIDE)
        inner = jnp.dot(f_ref[s, 0], g, preferred_element_type=jnp.float32)
        i_ref[s] = inner.astype(jnp.bfloat16)
    for s in slots:
        p_ref[s] = jnp.dot(i_ref[s], f_ref[s, 1], preferred_element_type=jnp.float32)
    ratio = []
    for s in slots:
        a_in[s].wait()
        adagrad = norm = jnp.zeros((8, SIDE), jnp.float32)
        for k in range(PEERS):
            rows = pl.ds(k * PIECE, PIECE)
            g = g_ref[k, s].astype(jnp.float32)
            squares = g * g
            accum = a_ref[s, rows] + squares
            ao_ref[s, rows] = accum
            adagrad += tile_sum(squares / accum)
            precond = p_ref[s, rows]
            norm += tile_sum(precond * precond)
        a_out[s].start()
        ratio.append(jnp.sqrt(jnp.sum(adagrad)) / jnp.sqrt(jnp.sum(norm) + 1e-06))
    for s in slots:
        for k in range(PEERS):
            rows = pl.ds(k * PIECE, PIECE)
            step = p_ref[s, rows] * ratio[s]
            moment = (0.9 * m_ref[s, rows].astype(jnp.float32) + step).astype(jnp.bfloat16)
            mo_ref[s, rows] = moment
            u_ref[k, s] = (0.9 * moment.astype(jnp.float32) + step).astype(jnp.bfloat16)
        m_out[s].start()
    for c in a_out + m_out:
        c.wait()


def slot_step(g, factors, momentum, accum):
    vmem, hbm = pl.BlockSpec(memory_space=pltpu.VMEM), pl.BlockSpec(memory_space=pltpu.HBM)
    slots = (SLOTS, SIDE, SIDE)
    return pl.pallas_call(
        slot_kernel,
        out_shape=(
            jax.ShapeDtypeStruct(slots, jnp.bfloat16),
            jax.ShapeDtypeStruct(slots, jnp.float32),
            jax.ShapeDtypeStruct(g.shape, jnp.bfloat16),
        ),
        in_specs=[vmem, vmem, vmem, hbm],
        out_specs=(hbm, hbm, vmem),
        scratch_shapes=[
            pltpu.VMEM(slots, jnp.float32),
            pltpu.VMEM(slots, jnp.float32),
            pltpu.VMEM(slots, jnp.bfloat16),
            pltpu.VMEM(slots, jnp.float32),
            pltpu.VMEM(slots, jnp.bfloat16),
            pltpu.SemaphoreType.DMA((SLOTS,)),
            pltpu.SemaphoreType.DMA((SLOTS,)),
            pltpu.SemaphoreType.DMA((SLOTS,)),
        ],
        compiler_params=pltpu.CompilerParams(vmem_limit_bytes=VMEM_LIMIT),
        name="slot_step",
    )(g, factors, momentum, accum)


def gather_replicas(tile, z, core):
    up1, down1 = up(tile[:HALF], "up1"), down(tile[HALF:], "down1")
    tile, own = lax.optimization_barrier((tile, swap(tile)))
    up2, down2 = up(tile[HALF:], "up2"), down(tile[:HALF], "down2")
    up3, down3 = up(up1, "up3"), down(down1, "down3")
    near = lax.optimization_barrier((up1, up2, down2, down1))
    other = [swap(x) for x in near]
    up3, down3, *other = lax.optimization_barrier((up3, down3, *other))
    out = jnp.zeros((SIDE, 8 * SIDE), tile.dtype)

    def put(out, x, row, d, which):
        return lax.dynamic_update_slice(out, x, (row, (lax.rem(z + d, 4) * 2 + which) * SIDE))

    out = put(put(out, tile, 0, 0, core), own, 0, 0, 1 - core)
    halves = [*zip(near, other), (up3, swap(up3)), (down3, swap(down3))]
    for n, (x, y) in enumerate(halves):
        row, d = n % 2 * HALF, (3, 1, 2)[n // 2]
        out = put(put(out, x, row, d, core), y, row, d, 1 - core)
    return out


def body(grads, owners, factors, momentum, accum):
    replica = lax.axis_index("replica")
    z, core = replica // 2, lax.rem(replica, 2)
    ids = owners[:, 0]
    named = ids[None, :] == jnp.arange(PEERS * SLOTS, dtype=jnp.int32)[:, None]
    block_of = jnp.max(
        jnp.where(named, jnp.arange(PEERS, dtype=jnp.int32)[None, :], -1), axis=1
    )

    home, block_of = sum_replicas(grads[0], z, core, block_of)
    pieces = lax.all_to_all(home.reshape(PEERS, PIECE, SIDE), "fsdp", 0, 0, tiled=True)
    routed = pick(block_of, pieces, PEERS * SLOTS)
    slot_grad = lax.all_to_all(
        routed.reshape(PEERS, SLOTS, PIECE, SIDE), "fsdp", 0, 0, tiled=True
    )
    moment_new, squares_new, update = slot_step(
        slot_grad, factors[0, 0], momentum[0, 0], accum[0, 0]
    )
    back = lax.all_to_all(update, "fsdp", 0, 0, tiled=True)
    back = pick(ids, back.reshape(PEERS * SLOTS, PIECE, SIDE), PEERS)
    tile = lax.all_to_all(back, "fsdp", 0, 0, tiled=True).reshape(SIDE, SIDE)
    out = gather_replicas(tile, z, core)
    return (out, moment_new[None, None], squares_new[None, None])


def solution(mesh):
    in_specs = (
        P("replica", "fsdp", None),
        P(None, "replica"),
        P("replica", "fsdp", None, None, None, None),
        P("replica", "fsdp", None, None, None),
        P("replica", "fsdp", None, None, None),
    )
    out_specs = (
        P("fsdp", None),
        P("replica", "fsdp", None, None, None),
        P("replica", "fsdp", None, None, None),
    )
    return jax.shard_map(body, mesh=mesh, in_specs=in_specs, out_specs=out_specs, check_vma=False)
```

```python
import jax
import jax.numpy as jnp
from jax import lax
from jax.experimental import pallas as pl
from jax.experimental.pallas import tpu as pltpu
from jax.sharding import PartitionSpec as P

SIDE = 512
SLOTS = 2
PEERS = 16
PIECE = SIDE // PEERS
VMEM_LIMIT = 24 * 1024 * 1024


NEXT = [(i, (i + 2) % 8) for i in range(0, 8, 2)]
CORES = [(i, i ^ 1) for i in range(8)]
PLANES = [[r * PEERS + f for r in range(c, 8, 2) for f in range(PEERS)] for c in range(2)]


def vmem_call(kernel, name, out_shape, *operands):
    spec = pl.BlockSpec(memory_space=pltpu.VMEM)
    return pl.pallas_call(
        kernel,
        out_shape=out_shape,
        in_specs=[spec] * len(operands),
        out_specs=jax.tree.map(lambda _: spec, out_shape),
        compiler_params=pltpu.CompilerParams(vmem_limit_bytes=VMEM_LIMIT),
        name=name,
    )(*operands)


def swap(x):
    with jax.named_scope("swap"):
        return lax.ppermute(x, "replica", CORES)


def exchange(x):
    return lax.all_to_all(
        x, ("replica", "fsdp"), 0, 0, tiled=True, axis_index_groups=PLANES
    )


def sum_kernel(a_ref, b_ref, after_ref, o_ref):
    for z in range(4):
        total = a_ref[z].astype(jnp.float32) + b_ref[z].astype(jnp.float32)
        o_ref[z] = total.astype(jnp.bfloat16)


def core_sums(grads, core):
    def part(z, which):
        return lax.dynamic_slice(grads, (0, (2 * z + which) * SIDE), (SIDE, SIDE))

    give = jnp.stack([part(z, 1 - core) for z in range(4)])
    got = swap(give)
    x = give[0, :16, :128]
    for _ in range(2):
        with jax.named_scope("hop"):
            x = lax.ppermute(x, "replica", NEXT)
    own = jnp.stack([part(z, core) for z in range(4)])
    return vmem_call(sum_kernel, "sum", jax.ShapeDtypeStruct(own.shape, own.dtype), own, got, x)


def pick_sum_kernel(index_ref, x_ref, o_ref):
    for t in range(o_ref.shape[0]):
        i = index_ref[t]
        at = jnp.maximum(i, 0)
        v = sum(x_ref[z * PEERS + at].astype(jnp.float32) for z in range(4))
        o_ref[t] = jnp.where(i >= 0, v, jnp.zeros_like(v)).astype(jnp.bfloat16)


def pick_copies_kernel(index_ref, x_ref, o_ref):
    for t in range(PEERS):
        v = x_ref[index_ref[t]]
        for z in range(4):
            o_ref[z * PEERS + t] = v


def pick(kernel, index, x, count):
    return pl.pallas_call(
        kernel,
        out_shape=jax.ShapeDtypeStruct((count,) + x.shape[1:], x.dtype),
        in_specs=[
            pl.BlockSpec(memory_space=pltpu.SMEM),
            pl.BlockSpec(memory_space=pltpu.VMEM),
        ],
        out_specs=pl.BlockSpec(memory_space=pltpu.VMEM),
        compiler_params=pltpu.CompilerParams(vmem_limit_bytes=VMEM_LIMIT),
        name="pick",
    )(index, x)


def tile_sum(x):
    return jnp.sum(x.reshape(-1, 8, SIDE), axis=0)


def slot_kernel(
    g_ref, f_ref, m_ref, a_hbm, mo_hbm, ao_hbm, u_ref,
    a_ref, ao_ref, mo_ref, p_ref, i_ref, a_sem, ao_sem, mo_sem,
):
    slots = range(SLOTS)
    a_in = [pltpu.make_async_copy(a_hbm.at[s], a_ref.at[s], a_sem.at[s]) for s in slots]
    a_out = [pltpu.make_async_copy(ao_ref.at[s], ao_hbm.at[s], ao_sem.at[s]) for s in slots]
    m_out = [pltpu.make_async_copy(mo_ref.at[s], mo_hbm.at[s], mo_sem.at[s]) for s in slots]
    for s in slots:
        a_in[s].start()
    for s in slots:
        g = g_ref[:, s].reshape(SIDE, SIDE)
        inner = jnp.dot(f_ref[s, 0], g, preferred_element_type=jnp.float32)
        i_ref[s] = inner.astype(jnp.bfloat16)
    for s in slots:
        p_ref[s] = jnp.dot(i_ref[s], f_ref[s, 1], preferred_element_type=jnp.float32)
    ratio = []
    for s in slots:
        a_in[s].wait()
        adagrad = norm = jnp.zeros((8, SIDE), jnp.float32)
        for k in range(PEERS):
            rows = pl.ds(k * PIECE, PIECE)
            g = g_ref[k, s].astype(jnp.float32)
            squares = g * g
            accum = a_ref[s, rows] + squares
            ao_ref[s, rows] = accum
            adagrad += tile_sum(squares / accum)
            precond = p_ref[s, rows]
            norm += tile_sum(precond * precond)
        a_out[s].start()
        ratio.append(jnp.sqrt(jnp.sum(adagrad)) / jnp.sqrt(jnp.sum(norm) + 1e-06))
    for s in slots:
        for k in range(PEERS):
            rows = pl.ds(k * PIECE, PIECE)
            step = p_ref[s, rows] * ratio[s]
            moment = (0.9 * m_ref[s, rows].astype(jnp.float32) + step).astype(jnp.bfloat16)
            mo_ref[s, rows] = moment
            u_ref[k, s] = (0.9 * moment.astype(jnp.float32) + step).astype(jnp.bfloat16)
        m_out[s].start()
    for c in a_out + m_out:
        c.wait()


def slot_step(g, factors, momentum, accum):
    vmem, hbm = pl.BlockSpec(memory_space=pltpu.VMEM), pl.BlockSpec(memory_space=pltpu.HBM)
    slots = (SLOTS, SIDE, SIDE)
    return pl.pallas_call(
        slot_kernel,
        out_shape=(
            jax.ShapeDtypeStruct(slots, jnp.bfloat16),
            jax.ShapeDtypeStruct(slots, jnp.float32),
            jax.ShapeDtypeStruct(g.shape, jnp.bfloat16),
        ),
        in_specs=[vmem, vmem, vmem, hbm],
        out_specs=(hbm, hbm, vmem),
        scratch_shapes=[
            pltpu.VMEM(slots, jnp.float32),
            pltpu.VMEM(slots, jnp.float32),
            pltpu.VMEM(slots, jnp.bfloat16),
            pltpu.VMEM(slots, jnp.float32),
            pltpu.VMEM(slots, jnp.bfloat16),
            pltpu.SemaphoreType.DMA((SLOTS,)),
            pltpu.SemaphoreType.DMA((SLOTS,)),
            pltpu.SemaphoreType.DMA((SLOTS,)),
        ],
        compiler_params=pltpu.CompilerParams(vmem_limit_bytes=VMEM_LIMIT),
        name="slot_step",
    )(g, factors, momentum, accum)


def gather_cores(blocks, core):
    other = swap(blocks)
    out = jnp.zeros((SIDE, 8 * SIDE), blocks.dtype)
    for z in range(4):
        out = lax.dynamic_update_slice(out, blocks[z], (0, (2 * z + core) * SIDE))
        out = lax.dynamic_update_slice(out, other[z], (0, (2 * z + 1 - core) * SIDE))
    return out


def body(grads, owners, factors, momentum, accum):
    core = lax.rem(lax.axis_index("replica"), 2)
    ids = owners[:, 0]
    named = ids[None, :] == jnp.arange(PEERS * SLOTS, dtype=jnp.int32)[:, None]
    block_of = jnp.max(
        jnp.where(named, jnp.arange(PEERS, dtype=jnp.int32)[None, :], -1), axis=1
    )

    sums = core_sums(grads[0], core)
    sums, block_of = lax.optimization_barrier((sums, block_of))
    pieces = exchange(sums.reshape(4 * PEERS, PIECE, SIDE))
    routed = pick(pick_sum_kernel, block_of, pieces, PEERS * SLOTS)
    slot_grad = lax.all_to_all(
        routed.reshape(PEERS, SLOTS, PIECE, SIDE), "fsdp", 0, 0, tiled=True
    )
    moment_new, squares_new, update = slot_step(
        slot_grad, factors[0, 0], momentum[0, 0], accum[0, 0]
    )
    back = lax.all_to_all(update, "fsdp", 0, 0, tiled=True)
    back = back.reshape(PEERS * SLOTS, PIECE, SIDE)
    blocks = exchange(pick(pick_copies_kernel, ids, back, 4 * PEERS))
    out = gather_cores(blocks.reshape(4, SIDE, SIDE), core)
    return (out, moment_new[None, None], squares_new[None, None])


def solution(mesh):
    in_specs = (
        P("replica", "fsdp", None),
        P(None, "replica"),
        P("replica", "fsdp", None, None, None, None),
        P("replica", "fsdp", None, None, None),
        P("replica", "fsdp", None, None, None),
    )
    out_specs = (
        P("fsdp", None),
        P("replica", "fsdp", None, None, None),
        P("replica", "fsdp", None, None, None),
    )
    return jax.shard_map(body, mesh=mesh, in_specs=in_specs, out_specs=out_specs, check_vma=False)
```

```python
import jax
import jax.numpy as jnp
from jax import lax
from jax.experimental import pallas as pl
from jax.experimental.pallas import tpu as pltpu
from jax.sharding import PartitionSpec as P

SIDE = 512
SLOTS = 2
PEERS = 16
PIECE = SIDE // PEERS
VMEM_LIMIT = 24 * 1024 * 1024


NEXT = [(i, i ^ 2) for i in range(0, 8, 2)]
CORES = [(i, i ^ 1) for i in range(8)]
PLANES = [[r * PEERS + f for r in range(c, 8, 2) for f in range(PEERS)] for c in range(2)]


def vmem_call(kernel, name, out_shape, *operands):
    spec = pl.BlockSpec(memory_space=pltpu.VMEM)
    return pl.pallas_call(
        kernel,
        out_shape=out_shape,
        in_specs=[spec] * len(operands),
        out_specs=jax.tree.map(lambda _: spec, out_shape),
        compiler_params=pltpu.CompilerParams(vmem_limit_bytes=VMEM_LIMIT),
        name=name,
    )(*operands)


def swap(x):
    with jax.named_scope("swap"):
        return lax.ppermute(x, "replica", CORES)


def exchange(x):
    return lax.all_to_all(
        x, ("replica", "fsdp"), 0, 0, tiled=True, axis_index_groups=PLANES
    )


def sum_kernel(own_ref, a_ref, b_ref, after_ref, o_ref):
    for z, other in enumerate((a_ref[0], a_ref[1], b_ref[0], b_ref[1])):
        total = own_ref[z].astype(jnp.float32) + other.astype(jnp.float32)
        o_ref[z] = total.astype(jnp.bfloat16)


def core_sums(grads, core):
    def part(x, z, which):
        return lax.dynamic_slice(x, (0, (2 * z + which) * SIDE), (SIDE, SIDE))

    give_a = jnp.stack([part(grads, z, 1 - core) for z in (0, 1)])
    later, give_a = lax.optimization_barrier((grads, give_a))
    got_a = swap(give_a)
    got_b = swap(jnp.stack([part(later, z, 1 - core) for z in (2, 3)]))
    x = give_a[0, :16, :128]
    for _ in range(2):
        with jax.named_scope("hop"):
            x = lax.ppermute(x, "replica", NEXT)
    own = jnp.stack([part(later, z, core) for z in range(4)])
    return vmem_call(sum_kernel, "sum", jax.ShapeDtypeStruct(own.shape, own.dtype), own, got_a, got_b, x)


def pick_sum_kernel(index_ref, x_ref, o_ref):
    for t in range(o_ref.shape[0]):
        i = index_ref[t]

        @pl.when(i >= 0)
        def _():
            v = sum(x_ref[z * PEERS + i].astype(jnp.float32) for z in range(4))
            o_ref[t] = v.astype(jnp.bfloat16)

        @pl.when(i < 0)
        def _():
            o_ref[t] = jnp.zeros_like(o_ref[t])


def pick_copies_kernel(index_ref, x_ref, o_ref):
    for t in range(PEERS):
        v = x_ref[index_ref[t]]
        for z in range(4):
            o_ref[z * PEERS + t] = v


def pick(kernel, index, x, count):
    return pl.pallas_call(
        kernel,
        out_shape=jax.ShapeDtypeStruct((count,) + x.shape[1:], x.dtype),
        in_specs=[
            pl.BlockSpec(memory_space=pltpu.SMEM),
            pl.BlockSpec(memory_space=pltpu.VMEM),
        ],
        out_specs=pl.BlockSpec(memory_space=pltpu.VMEM),
        compiler_params=pltpu.CompilerParams(vmem_limit_bytes=VMEM_LIMIT),
        name="pick",
    )(index, x)


def tile_sum(x):
    return jnp.sum(x.reshape(-1, 8, SIDE), axis=0)


def slot_kernel(
    g_ref, f_ref, m_ref, a_hbm, mo_hbm, ao_hbm, u_ref,
    a_ref, ao_ref, mo_ref, p_ref, i_ref, a_sem, ao_sem, mo_sem,
):
    slots = range(SLOTS)
    a_in = [pltpu.make_async_copy(a_hbm.at[s], a_ref.at[s], a_sem.at[s]) for s in slots]
    a_out = [pltpu.make_async_copy(ao_ref.at[s], ao_hbm.at[s], ao_sem.at[s]) for s in slots]
    m_out = [pltpu.make_async_copy(mo_ref.at[s], mo_hbm.at[s], mo_sem.at[s]) for s in slots]
    for s in slots:
        a_in[s].start()
    for s in slots:
        g = g_ref[:, s].reshape(SIDE, SIDE)
        inner = jnp.dot(f_ref[s, 0], g, preferred_element_type=jnp.float32)
        i_ref[s] = inner.astype(jnp.bfloat16)
    for s in slots:
        p_ref[s] = jnp.dot(i_ref[s], f_ref[s, 1], preferred_element_type=jnp.float32)
    ratio = []
    for s in slots:
        a_in[s].wait()
        adagrad = norm = jnp.zeros((8, SIDE), jnp.float32)
        for k in range(PEERS):
            rows = pl.ds(k * PIECE, PIECE)
            g = g_ref[k, s].astype(jnp.float32)
            squares = g * g
            accum = a_ref[s, rows] + squares
            ao_ref[s, rows] = accum
            adagrad += tile_sum(squares / accum)
            precond = p_ref[s, rows]
            norm += tile_sum(precond * precond)
        a_out[s].start()
        ratio.append(jnp.sqrt(jnp.sum(adagrad)) / jnp.sqrt(jnp.sum(norm) + 1e-06))
    for s in slots:
        for k in range(PEERS):
            rows = pl.ds(k * PIECE, PIECE)
            step = p_ref[s, rows] * ratio[s]
            moment = (0.9 * m_ref[s, rows].astype(jnp.float32) + step).astype(jnp.bfloat16)
            mo_ref[s, rows] = moment
            u_ref[k, s] = (0.9 * moment.astype(jnp.float32) + step).astype(jnp.bfloat16)
        m_out[s].start()
    for c in a_out + m_out:
        c.wait()


def slot_step(g, factors, momentum, accum):
    vmem, hbm = pl.BlockSpec(memory_space=pltpu.VMEM), pl.BlockSpec(memory_space=pltpu.HBM)
    slots = (SLOTS, SIDE, SIDE)
    return pl.pallas_call(
        slot_kernel,
        out_shape=(
            jax.ShapeDtypeStruct(slots, jnp.bfloat16),
            jax.ShapeDtypeStruct(slots, jnp.float32),
            jax.ShapeDtypeStruct(g.shape, jnp.bfloat16),
        ),
        in_specs=[vmem, vmem, vmem, hbm],
        out_specs=(hbm, hbm, vmem),
        scratch_shapes=[
            pltpu.VMEM(slots, jnp.float32),
            pltpu.VMEM(slots, jnp.float32),
            pltpu.VMEM(slots, jnp.bfloat16),
            pltpu.VMEM(slots, jnp.float32),
            pltpu.VMEM(slots, jnp.bfloat16),
            pltpu.SemaphoreType.DMA((SLOTS,)),
            pltpu.SemaphoreType.DMA((SLOTS,)),
            pltpu.SemaphoreType.DMA((SLOTS,)),
        ],
        compiler_params=pltpu.CompilerParams(vmem_limit_bytes=VMEM_LIMIT),
        name="slot_step",
    )(g, factors, momentum, accum)


def store_kernel(cols_ref, x_ref, *refs):
    o_ref, sems = refs[-2:]
    copies = []
    for n in range(x_ref.shape[0]):
        to = o_ref.at[:, pl.ds(pl.multiple_of(cols_ref[n] * SIDE, SIDE), SIDE)]
        copies.append(pltpu.make_async_copy(x_ref.at[n], to, sems.at[n]))
    for c in copies:
        c.start()
    for c in copies:
        c.wait()


def store(x, cols, *out):
    hbm = pl.BlockSpec(memory_space=pltpu.HBM)
    specs = [pl.BlockSpec(memory_space=pltpu.SMEM), pl.BlockSpec(memory_space=pltpu.VMEM)]
    return pl.pallas_call(
        store_kernel,
        out_shape=jax.ShapeDtypeStruct((SIDE, 8 * SIDE), x.dtype),
        in_specs=specs + [hbm] * len(out),
        out_specs=hbm,
        scratch_shapes=[pltpu.SemaphoreType.DMA((x.shape[0],))],
        input_output_aliases={2: 0} if out else {},
        compiler_params=pltpu.CompilerParams(vmem_limit_bytes=VMEM_LIMIT),
        name="store",
    )(jnp.stack(cols), x, *out)


def gather_cores(blocks, core):
    first, second = swap(blocks[:2]), swap(blocks[2:])
    out = store(blocks, [2 * z + core for z in range(4)])
    out = store(first, [2 * z + 1 - core for z in (0, 1)], out)
    return store(second, [2 * z + 1 - core for z in (2, 3)], out)


def body(grads, owners, factors, momentum, accum):
    core = lax.rem(lax.axis_index("replica"), 2)
    ids = owners[:, 0]
    named = ids[None, :] == jnp.arange(PEERS * SLOTS, dtype=jnp.int32)[:, None]
    block_of = jnp.max(
        jnp.where(named, jnp.arange(PEERS, dtype=jnp.int32)[None, :], -1), axis=1
    )

    sums = core_sums(grads[0], core)
    sums, block_of = lax.optimization_barrier((sums, block_of))
    pieces = exchange(sums.reshape(4 * PEERS, PIECE, SIDE))
    routed = pick(pick_sum_kernel, block_of, pieces, PEERS * SLOTS)
    slot_grad = lax.all_to_all(
        routed.reshape(PEERS, SLOTS, PIECE, SIDE), "fsdp", 0, 0, tiled=True
    )
    moment_new, squares_new, update = slot_step(
        slot_grad, factors[0, 0], momentum[0, 0], accum[0, 0]
    )
    back = lax.all_to_all(update, "fsdp", 0, 0, tiled=True)
    back = back.reshape(PEERS * SLOTS, PIECE, SIDE)
    blocks = exchange(pick(pick_copies_kernel, ids, back, 4 * PEERS))
    out = gather_cores(blocks.reshape(4, SIDE, SIDE), core)
    return (out, moment_new[None, None], squares_new[None, None])


def solution(mesh):
    in_specs = (
        P("replica", "fsdp", None),
        P(None, "replica"),
        P("replica", "fsdp", None, None, None, None),
        P("replica", "fsdp", None, None, None),
        P("replica", "fsdp", None, None, None),
    )
    out_specs = (
        P("fsdp", None),
        P("replica", "fsdp", None, None, None),
        P("replica", "fsdp", None, None, None),
    )
    return jax.shard_map(body, mesh=mesh, in_specs=in_specs, out_specs=out_specs, check_vma=False)
```

```python
import jax
import jax.numpy as jnp
from jax import lax
from jax.experimental import pallas as pl
from jax.experimental.pallas import tpu as pltpu
from jax.sharding import PartitionSpec as P

SIDE = 512
SLOTS = 2
PEERS = 16
PIECE = SIDE // PEERS
VMEM_LIMIT = 24 * 1024 * 1024


NEXT = [(i, i ^ 2) for i in range(0, 8, 2)]
CORES = [(i, i ^ 1) for i in range(8)]
PLANES = [[r * PEERS + f for r in range(c, 8, 2) for f in range(PEERS)] for c in range(2)]


def vmem_call(kernel, name, out_shape, *operands):
    spec = pl.BlockSpec(memory_space=pltpu.VMEM)
    return pl.pallas_call(
        kernel,
        out_shape=out_shape,
        in_specs=[spec] * len(operands),
        out_specs=jax.tree.map(lambda _: spec, out_shape),
        compiler_params=pltpu.CompilerParams(vmem_limit_bytes=VMEM_LIMIT),
        name=name,
    )(*operands)


def swap(x):
    with jax.named_scope("swap"):
        return lax.ppermute(x, "replica", CORES)


def exchange(x):
    return lax.all_to_all(
        x, ("replica", "fsdp"), 0, 0, tiled=True, axis_index_groups=PLANES
    )


def sum_kernel(*refs):
    o_ref = refs[-1]
    for z in range(4):
        total = refs[z][...].astype(jnp.float32) + refs[4 + z][...].astype(jnp.float32)
        o_ref[z] = total.astype(jnp.bfloat16)


def core_sums(grads, core):
    def part(x, z, which):
        return lax.dynamic_slice(x, (0, (2 * z + which) * SIDE), (SIDE, SIDE))

    give_a = [part(grads, z, 1 - core) for z in (0, 1)]
    later, *give_a = lax.optimization_barrier((grads, *give_a))
    got = [swap(x) for x in give_a + [part(later, z, 1 - core) for z in (2, 3)]]
    x = give_a[0][:16, :128]
    for _ in range(2):
        with jax.named_scope("hop"):
            x = lax.ppermute(x, "replica", NEXT)
    own = [part(later, z, core) for z in range(4)]
    shape = jax.ShapeDtypeStruct((4, SIDE, SIDE), grads.dtype)
    return vmem_call(sum_kernel, "sum", shape, *own, *got, x)


def pick_sum_kernel(index_ref, x_ref, o_ref):
    for t in range(o_ref.shape[0]):
        i = index_ref[t]

        @pl.when(i >= 0)
        def _():
            v = sum(x_ref[z * PEERS + i].astype(jnp.float32) for z in range(4))
            o_ref[t] = v.astype(jnp.bfloat16)

        @pl.when(i < 0)
        def _():
            o_ref[t] = jnp.zeros_like(o_ref[t])


def pick_copies_kernel(index_ref, x_ref, o_ref):
    for t in range(PEERS):
        v = x_ref[index_ref[t]]
        for z in range(4):
            o_ref[z * PEERS + t] = v


def pick(kernel, index, x, count):
    return pl.pallas_call(
        kernel,
        out_shape=jax.ShapeDtypeStruct((count,) + x.shape[1:], x.dtype),
        in_specs=[
            pl.BlockSpec(memory_space=pltpu.SMEM),
            pl.BlockSpec(memory_space=pltpu.VMEM),
        ],
        out_specs=pl.BlockSpec(memory_space=pltpu.VMEM),
        compiler_params=pltpu.CompilerParams(vmem_limit_bytes=VMEM_LIMIT),
        name="pick",
    )(index, x)


def tile_sum(x):
    return jnp.sum(x.reshape(-1, 8, SIDE), axis=0)


def slot_kernel(
    g_ref, f_ref, m_ref, a_hbm, mo_hbm, ao_hbm, u_ref,
    a_ref, ao_ref, mo_ref, p_ref, i_ref, a_sem, ao_sem, mo_sem,
):
    slots = range(SLOTS)
    a_in = [pltpu.make_async_copy(a_hbm.at[s], a_ref.at[s], a_sem.at[s]) for s in slots]
    a_out = [pltpu.make_async_copy(ao_ref.at[s], ao_hbm.at[s], ao_sem.at[s]) for s in slots]
    m_out = [pltpu.make_async_copy(mo_ref.at[s], mo_hbm.at[s], mo_sem.at[s]) for s in slots]
    for s in slots:
        a_in[s].start()
    for s in slots:
        g = g_ref[:, s].reshape(SIDE, SIDE)
        inner = jnp.dot(f_ref[s, 0], g, preferred_element_type=jnp.float32)
        i_ref[s] = inner.astype(jnp.bfloat16)
    for s in slots:
        p_ref[s] = jnp.dot(i_ref[s], f_ref[s, 1], preferred_element_type=jnp.float32)
    ratio = []
    for s in slots:
        a_in[s].wait()
        adagrad = norm = jnp.zeros((8, SIDE), jnp.float32)
        for k in range(PEERS):
            rows = pl.ds(k * PIECE, PIECE)
            g = g_ref[k, s].astype(jnp.float32)
            squares = g * g
            accum = a_ref[s, rows] + squares
            ao_ref[s, rows] = accum
            adagrad += tile_sum(squares / accum)
            precond = p_ref[s, rows]
            norm += tile_sum(precond * precond)
        a_out[s].start()
        ratio.append(jnp.sqrt(jnp.sum(adagrad)) / jnp.sqrt(jnp.sum(norm) + 1e-06))
    for s in slots:
        for k in range(PEERS):
            rows = pl.ds(k * PIECE, PIECE)
            step = p_ref[s, rows] * ratio[s]
            moment = (0.9 * m_ref[s, rows].astype(jnp.float32) + step).astype(jnp.bfloat16)
            mo_ref[s, rows] = moment
            u_ref[k, s] = (0.9 * moment.astype(jnp.float32) + step).astype(jnp.bfloat16)
        m_out[s].start()
    for c in a_out + m_out:
        c.wait()


def slot_step(g, factors, momentum, accum):
    vmem, hbm = pl.BlockSpec(memory_space=pltpu.VMEM), pl.BlockSpec(memory_space=pltpu.HBM)
    slots = (SLOTS, SIDE, SIDE)
    return pl.pallas_call(
        slot_kernel,
        out_shape=(
            jax.ShapeDtypeStruct(slots, jnp.bfloat16),
            jax.ShapeDtypeStruct(slots, jnp.float32),
            jax.ShapeDtypeStruct(g.shape, jnp.bfloat16),
        ),
        in_specs=[vmem, vmem, vmem, hbm],
        out_specs=(hbm, hbm, vmem),
        scratch_shapes=[
            pltpu.VMEM(slots, jnp.float32),
            pltpu.VMEM(slots, jnp.float32),
            pltpu.VMEM(slots, jnp.bfloat16),
            pltpu.VMEM(slots, jnp.float32),
            pltpu.VMEM(slots, jnp.bfloat16),
            pltpu.SemaphoreType.DMA((SLOTS,)),
            pltpu.SemaphoreType.DMA((SLOTS,)),
            pltpu.SemaphoreType.DMA((SLOTS,)),
        ],
        compiler_params=pltpu.CompilerParams(vmem_limit_bytes=VMEM_LIMIT),
        name="slot_step",
    )(g, factors, momentum, accum)


def store_kernel(cols_ref, x_ref, *refs):
    o_ref, sems = refs[-2:]
    copies = []
    for n in range(x_ref.shape[0]):
        to = o_ref.at[:, pl.ds(pl.multiple_of(cols_ref[n] * SIDE, SIDE), SIDE)]
        copies.append(pltpu.make_async_copy(x_ref.at[n], to, sems.at[n]))
    for c in copies:
        c.start()
    for c in copies:
        c.wait()


def store(x, cols, *out):
    hbm = pl.BlockSpec(memory_space=pltpu.HBM)
    specs = [pl.BlockSpec(memory_space=pltpu.SMEM), pl.BlockSpec(memory_space=pltpu.VMEM)]
    return pl.pallas_call(
        store_kernel,
        out_shape=jax.ShapeDtypeStruct((SIDE, 8 * SIDE), x.dtype),
        in_specs=specs + [hbm] * len(out),
        out_specs=hbm,
        scratch_shapes=[pltpu.SemaphoreType.DMA((x.shape[0],))],
        input_output_aliases={2: 0} if out else {},
        compiler_params=pltpu.CompilerParams(vmem_limit_bytes=VMEM_LIMIT),
        name="store",
    )(jnp.stack(cols), x, *out)


def gather_cores(blocks, core):
    first, second = swap(blocks[:2]), swap(blocks[2:])
    out = store(blocks, [2 * z + core for z in range(4)])
    out = store(first, [2 * z + 1 - core for z in (0, 1)], out)
    return store(second, [2 * z + 1 - core for z in (2, 3)], out)


def body(grads, owners, factors, momentum, accum):
    core = lax.rem(lax.axis_index("replica"), 2)
    ids = owners[:, 0]
    named = ids[None, :] == jnp.arange(PEERS * SLOTS, dtype=jnp.int32)[:, None]
    block_of = jnp.max(
        jnp.where(named, jnp.arange(PEERS, dtype=jnp.int32)[None, :], -1), axis=1
    )

    sums = core_sums(grads[0], core)
    sums, block_of = lax.optimization_barrier((sums, block_of))
    pieces = exchange(sums.reshape(4 * PEERS, PIECE, SIDE))
    routed = pick(pick_sum_kernel, block_of, pieces, PEERS * SLOTS)
    slot_grad = lax.all_to_all(
        routed.reshape(PEERS, SLOTS, PIECE, SIDE), "fsdp", 0, 0, tiled=True
    )
    moment_new, squares_new, update = slot_step(
        slot_grad, factors[0, 0], momentum[0, 0], accum[0, 0]
    )
    back = lax.all_to_all(update, "fsdp", 0, 0, tiled=True)
    back = back.reshape(PEERS * SLOTS, PIECE, SIDE)
    blocks = exchange(pick(pick_copies_kernel, ids, back, 4 * PEERS))
    out = gather_cores(blocks.reshape(4, SIDE, SIDE), core)
    return (out, moment_new[None, None], squares_new[None, None])


def solution(mesh):
    in_specs = (
        P("replica", "fsdp", None),
        P(None, "replica"),
        P("replica", "fsdp", None, None, None, None),
        P("replica", "fsdp", None, None, None),
        P("replica", "fsdp", None, None, None),
    )
    out_specs = (
        P("fsdp", None),
        P("replica", "fsdp", None, None, None),
        P("replica", "fsdp", None, None, None),
    )
    return jax.shard_map(body, mesh=mesh, in_specs=in_specs, out_specs=out_specs, check_vma=False)
```
